32 devices in a mesh: ty: 4 (over x, core), tx: 4 (over z), mode: 2 (over y).
Axes of the slice: x: 2, y: 2, z: 4, core: 2. Of those that a mesh axis runs over, the one named last changes fastest.
Arguments:
- object_field: float32 [2, 2, 1024, 1024], P(None, None, 'ty', 'tx'), may hold values from -2.4 to 2.4
- probe: float32 [4, 256, 512], P('mode'), may hold values from -6 to 6
- patterns: float32 [16, 256, 256], P(('ty', 'tx')), may hold values from 0.2 to 3
- offsets: int32 [16, 2], P(('ty', 'tx')), may hold values from 0 to 128
- phase: float32 [256, 256], replicated, may hold values from -3.140625 to 3.140625
- past_steps: bfloat16 [5, 2, 2, 1024, 1024], P(None, None, None, 'ty', 'tx'), may hold values from -4 to 4
- past_changes: bfloat16 [5, 2, 2, 1024, 1024], P(None, None, None, 'ty', 'tx'), may hold values from -16 to 16, as said below
Outputs:
- new_object: float32 [2, 2, 1024, 1024], P(None, None, 'ty', 'tx')
- gradient: float32 [2, 2, 1024, 1024], P(None, None, 'ty', 'tx')
The draws below stay inside these ranges and needn't reach their ends.
Inputs may be any that keep to these rules, and one draw needn't show every extreme that they name: Every entry of past_changes has the sign of the same entry of past_steps.
All inputs are finite; a program needn't handle non-finite values.
Results may differ from the reference program's by a relative error of at most 0.02.
Values sent between devices are 32-bit elements; how exact they have to be, the bound alone decides.
A program may use at most 64 MiB of HBM per device.

```python
import math
import jax
import jax.numpy as jnp
from jax import lax

PROBE = 256
MODES = 4
SLICES = 2
MEMORY = 5
TILE = 256
HALO = 64
P_DEV = 1
NY = 1024
NX = 1024
NPAT = 16
SPAN = 128
N_TX = 4


def object_base(key):
    object_key = jax.random.fold_in(key, 101)
    return 0.6 * jax.random.truncated_normal(object_key, -4.0, 4.0, (SLICES, 2, NY, NX), jnp.float32)


def history_steps(key):
    base = object_base(key)
    row_key = jax.random.fold_in(key, 202)
    col_key = jax.random.fold_in(key, 203)
    noise_key = jax.random.fold_in(key, 204)
    low_scale, high_scale = (0.3, 3.0)
    row_scale = jnp.exp(jax.random.uniform(row_key, (MEMORY, 1, 1, NY, 1), jnp.float32, math.log(low_scale), math.log(high_scale)))
    col_scale = jnp.exp(jax.random.uniform(col_key, (MEMORY, 1, 1, 1, NX), jnp.float32, math.log(low_scale), math.log(high_scale)))
    own_noise = jax.random.truncated_normal(noise_key, -4.0, 4.0, (MEMORY, SLICES, 2, NY, NX), jnp.float32)
    noise = own_noise
    return 0.3 * (base[None] + 0.3 * noise * row_scale * col_scale)


def draw_object_field(key, part):
    return object_base(key)


def draw_past_steps(key, part):
    return history_steps(key).astype(jnp.bfloat16)


def draw_past_changes(key, part):
    steps = history_steps(key).astype(jnp.bfloat16).astype(jnp.float32)
    curvature = jnp.exp(jax.random.uniform(jax.random.fold_in(key, 303), steps.shape, jnp.float32, math.log(0.5), math.log(4.0)))
    return (curvature * steps).astype(jnp.bfloat16)


def with_ends(array, rng, low, largest):
    longest = array.shape.index(max(array.shape))
    spots = []
    for shift in (0, 1):
        where = [jax.random.randint(jax.random.fold_in(rng, axis), (), 0, length) for axis, length in enumerate(array.shape)]
        where[longest] = (where[longest] + shift) % array.shape[longest]
        spots.append(tuple(where))
    return array.at[spots[0]].set(low).at[spots[1]].set(largest)


def block_levels(stream_key, extent, cuts, low, high):
    factor_of, own = 1.0, jax.random.fold_in(stream_key, 6)
    for position, parts in cuts:
        steps = jnp.exp(jax.random.uniform(jax.random.fold_in(own, position), (parts,), jnp.float32, low / len(cuts), high / len(cuts)))
        factor_of = factor_of * jnp.repeat(steps, extent[position] // parts).reshape([-1 if axis == position else 1 for axis in range(len(extent))])
    return factor_of


def gaussian(key, extent, scale, reach, split=(), held_as=jnp.bfloat16):
    values = scale * jax.random.normal(key, extent, jnp.float32)
    if split:
        values = values * block_levels(key, extent, split, -0.22, 0.18)
    return jnp.clip(values, -reach, reach).astype(held_as)


def setup_inputs(seed: int = 0) -> dict:
    splits = jax.random.split(jax.random.key(seed), 8)
    object_field = draw_object_field(jax.random.fold_in(splits[7], 71), 0)
    probe = gaussian(splits[1], (MODES, PROBE, 2 * PROBE), 1.0, 6.0, ((0, 2),), jnp.float32)
    patterns = jnp.clip(jnp.exp(math.log(3.0) - 2.7080502 * jax.random.uniform(splits[2], (NPAT, PROBE, PROBE), jnp.float32) ** block_levels(splits[2], (NPAT, PROBE, PROBE), ((0, 16),), -0.2, 0.2)), 0.2, 3.0)
    offsets = with_ends(jax.random.randint(splits[3], (NPAT, 2), 0, SPAN + 1), jax.random.fold_in(splits[3], 1), 0, SPAN).astype(jnp.int32)
    phase = jnp.clip(jax.random.uniform(splits[4], (PROBE, PROBE), jnp.float32, -3.140625, 3.140625), -3.140625, 3.140625)
    past_steps = draw_past_steps(jax.random.fold_in(splits[7], 71), 0)
    past_changes = draw_past_changes(jax.random.fold_in(splits[7], 71), 0)
    return dict(object_field=object_field, probe=probe, patterns=patterns, offsets=offsets, phase=phase, past_steps=past_steps, past_changes=past_changes)


REG_WEIGHT = 1.0

def dft_tables(length):
    indices = jnp.arange(length, dtype=jnp.int32)
    products = indices[:, None] * indices[None, :] % length
    angles = products.astype(jnp.float32) * (2.0 * math.pi / length)
    cosine_table = jnp.cos(angles) / math.sqrt(length)
    sine_table = jnp.sin(angles) / math.sqrt(length)
    forward_right = jnp.concatenate([jnp.concatenate([cosine_table, -sine_table], 1), jnp.concatenate([sine_table, cosine_table], 1)], 0)
    inverse_right = jnp.concatenate([jnp.concatenate([cosine_table, sine_table], 1), jnp.concatenate([-sine_table, cosine_table], 1)], 0)
    left_table = jnp.concatenate([cosine_table, sine_table], 0)
    return (forward_right.astype(jnp.bfloat16), inverse_right.astype(jnp.bfloat16), left_table.astype(jnp.bfloat16))

def transform(wavefield, tables, inverse):
    right_table = tables[1] if inverse else tables[0]
    sign_value = -1.0 if inverse else 1.0
    lead_shape = wavefield.shape[:-2]
    length = wavefield.shape[-2]
    flat_wave = wavefield.reshape(-1, 2 * length).astype(jnp.bfloat16)
    first_pass = jnp.dot(flat_wave, right_table, preferred_element_type=jnp.float32)
    first_pass = first_pass.reshape(-1, length, 2 * length).astype(jnp.bfloat16)
    second_pass = jnp.einsum('jk,bkl->bjl', tables[2].astype(jnp.float32), first_pass.astype(jnp.float32), precision=lax.Precision.HIGHEST)
    upper = second_pass[:, :length]
    lower = second_pass[:, length:]
    real_part = upper[:, :, :length] + sign_value * lower[:, :, length:]
    imag_part = upper[:, :, length:] - sign_value * lower[:, :, :length]
    return jnp.concatenate([real_part, imag_part], -1).reshape(lead_shape + (length, 2 * length))

def complex_product(first, second, conjugate_first):
    length = first.shape[-1] // 2
    first_real = first[..., :length]
    first_imag = first[..., length:]
    if conjugate_first:
        first_imag = -first_imag
    second_real = second[..., :length]
    second_imag = second[..., length:]
    return jnp.concatenate([first_real * second_real - first_imag * second_imag, first_real * second_imag + first_imag * second_real], -1)

def propagate(wavefield, kernel, tables, adjoint):
    spectrum = transform(wavefield, tables, False)
    spectrum = complex_product(kernel, spectrum, adjoint)
    return transform(spectrum, tables, True)

def forward_waves(windows, probe, kernel, tables):
    slice_count = windows.shape[1]
    wavefield = jnp.broadcast_to(probe[None], (windows.shape[0],) + probe.shape)
    entering = []
    for slice_index in range(slice_count):
        entering.append(wavefield)
        wavefield = complex_product(windows[:, slice_index][:, None], wavefield, False)
        if slice_index + 1 < slice_count:
            wavefield = propagate(wavefield, kernel, tables, False)
    return (transform(wavefield, tables, False), entering)

def window_gradients(far_field, entering, windows, residual, kernel, tables):
    slice_count = windows.shape[1]
    doubled = jnp.concatenate([residual, residual], -1)[:, None]
    adjoint_wave = transform(2.0 / MODES * doubled * far_field, tables, True)
    pieces = []
    for slice_index in reversed(range(slice_count)):
        pieces.append(lax.optimization_barrier(jnp.sum(complex_product(entering[slice_index], adjoint_wave, True), axis=1)))
        if slice_index > 0:
            adjoint_wave = complex_product(windows[:, slice_index][:, None], adjoint_wave, True)
            adjoint_wave = propagate(adjoint_wave, kernel, tables, True)
    return jnp.stack(pieces[::-1], 1)

def inner_product(first, second):
    return jnp.sum(first.astype(jnp.float32) * second.astype(jnp.float32))

def reference(object_field, probe, patterns, offsets, phase, past_steps, past_changes):
    probe_edge = probe.shape[1]
    rows_total = object_field.shape[2]
    cols_total = object_field.shape[3]
    tables = dft_tables(probe_edge)
    kernel = jnp.concatenate([jnp.cos(phase), jnp.sin(phase)], -1)
    span_ids = jnp.arange(probe_edge, dtype=jnp.int32)

    def one_pattern(collected, inputs):
        pattern, offset, pattern_index = inputs
        device = pattern_index // P_DEV
        row_start = TILE * (device // N_TX) - HALO + offset[0]
        col_start = TILE * (device % N_TX) - HALO + offset[1]
        row_ids = ((row_start + span_ids) % rows_total).astype(jnp.int32)
        col_ids = ((col_start + span_ids) % cols_total).astype(jnp.int32)
        window = object_field[:, :, row_ids[:, None], col_ids[None, :]]
        packed = jnp.concatenate([window[:, 0], window[:, 1]], -1)[None]
        far_field, entering = forward_waves(packed, probe, kernel, tables)
        intensity = lax.optimization_barrier(jnp.sum(far_field[..., :probe_edge] ** 2 + far_field[..., probe_edge:] ** 2, axis=1)) / MODES
        residual = intensity - pattern[None]
        pieces = window_gradients(far_field, entering, packed, residual, kernel, tables)[0]
        unpacked = jnp.stack([pieces[..., :probe_edge], pieces[..., probe_edge:]], 1)
        collected = collected.at[:, :, row_ids[:, None], col_ids[None, :]].add(unpacked)
        return (collected, None)
    zero_field = jnp.zeros(object_field.shape, jnp.float32)
    pattern_ids = jnp.arange(patterns.shape[0], dtype=jnp.int32)
    collected, unused = lax.scan(one_pattern, zero_field, (patterns, offsets, pattern_ids))
    gradient = collected + REG_WEIGHT * object_field
    memory = past_steps.shape[0]
    curvatures = [inner_product(past_steps[history_index], past_changes[history_index]) for history_index in range(memory)]
    search = gradient
    alphas = [None] * memory
    for history_index in reversed(range(memory)):
        alphas[history_index] = inner_product(past_steps[history_index], search) / curvatures[history_index]
        search = search - alphas[history_index] * past_changes[history_index].astype(jnp.float32)
    scaling = curvatures[memory - 1] / inner_product(past_changes[memory - 1], past_changes[memory - 1])
    search = scaling * search
    for history_index in range(memory):
        beta_value = inner_product(past_changes[history_index], search) / curvatures[history_index]
        search = search + (alphas[history_index] - beta_value) * past_steps[history_index].astype(jnp.float32)
    new_object = object_field - search
    return (new_object, gradient)
```

```python
import math

import jax
import jax.numpy as jnp
from jax import lax
from jax.sharding import PartitionSpec as P

MODES = 4
HALO = 64


REG_WEIGHT = 1.0


def extended_2(value, sides, width):
    for axis, dim in sides:
        size, length = (lax.axis_size(axis), value.shape[dim])
        up = [(i, (i + 1) % size) for i in range(size)]
        down = [(j, i) for i, j in up]
        last = lax.slice_in_dim(value, length - width, length, axis=dim)
        first = lax.slice_in_dim(value, 0, width, axis=dim)
        before = lax.ppermute(last, axis, up)
        after = lax.ppermute(first, axis, down)
        value = jnp.concatenate([before, value, after], axis=dim)
    return value


def dft_tables(length):
    indices = jnp.arange(length, dtype=jnp.int32)
    products = indices[:, None] * indices[None, :] % length
    angles = products.astype(jnp.float32) * (2.0 * math.pi / length)
    cosine_table = jnp.cos(angles) / math.sqrt(length)
    sine_table = jnp.sin(angles) / math.sqrt(length)
    forward_right = jnp.concatenate(
        [
            jnp.concatenate([cosine_table, -sine_table], 1),
            jnp.concatenate([sine_table, cosine_table], 1),
        ],
        0,
    )
    inverse_right = jnp.concatenate(
        [
            jnp.concatenate([cosine_table, sine_table], 1),
            jnp.concatenate([-sine_table, cosine_table], 1),
        ],
        0,
    )
    left_table = jnp.concatenate([cosine_table, sine_table], 0)
    return (
        forward_right.astype(jnp.bfloat16),
        inverse_right.astype(jnp.bfloat16),
        left_table.astype(jnp.bfloat16),
    )


def transform(wavefield, tables, inverse):
    right_table = tables[1] if inverse else tables[0]
    sign_value = -1.0 if inverse else 1.0
    lead_shape = wavefield.shape[:-2]
    length = wavefield.shape[-2]
    flat_wave = wavefield.reshape(-1, 2 * length).astype(jnp.bfloat16)
    first_pass = jnp.dot(flat_wave, right_table, preferred_element_type=jnp.float32)
    first_pass = first_pass.reshape(-1, length, 2 * length).astype(jnp.bfloat16)
    second_pass = jnp.einsum(
        "jk,bkl->bjl", tables[2], first_pass, preferred_element_type=jnp.float32
    )
    upper = second_pass[:, :length]
    lower = second_pass[:, length:]
    real_part = upper[:, :, :length] + sign_value * lower[:, :, length:]
    imag_part = upper[:, :, length:] - sign_value * lower[:, :, :length]
    return jnp.concatenate([real_part, imag_part], -1).reshape(lead_shape + (length, 2 * length))


def complex_product(first, second, conjugate_first):
    length = first.shape[-1] // 2
    first_real = first[..., :length]
    first_imag = first[..., length:]
    if conjugate_first:
        first_imag = -first_imag
    second_real = second[..., :length]
    second_imag = second[..., length:]
    return jnp.concatenate(
        [
            first_real * second_real - first_imag * second_imag,
            first_real * second_imag + first_imag * second_real,
        ],
        -1,
    )


def propagate(wavefield, kernel, tables, adjoint):
    spectrum = transform(wavefield, tables, False)
    spectrum = complex_product(kernel, spectrum, adjoint)
    return transform(spectrum, tables, True)


def forward_waves(windows, probe, kernel, tables):
    slice_count = windows.shape[1]
    wavefield = probe[None]
    entering = []
    for slice_index in range(slice_count):
        entering.append(wavefield)
        wavefield = complex_product(windows[:, slice_index][:, None], wavefield, False)
        if slice_index + 1 < slice_count:
            wavefield = propagate(wavefield, kernel, tables, False)
    return (transform(wavefield, tables, False), entering)


def window_gradients(far_field, entering, windows, residual, kernel, tables):
    slice_count = windows.shape[1]
    doubled = jnp.concatenate([residual, residual], -1)[:, None]
    adjoint_wave = transform(2.0 / MODES * doubled * far_field, tables, True)
    pieces = []
    for slice_index in reversed(range(slice_count)):
        piece = jnp.sum(complex_product(entering[slice_index], adjoint_wave, True), axis=1)
        pieces.append(axis_sum(piece, "mode"))
        if slice_index > 0:
            adjoint_wave = complex_product(windows[:, slice_index][:, None], adjoint_wave, True)
            adjoint_wave = propagate(adjoint_wave, kernel, tables, True)
    return jnp.stack(pieces[::-1], 1)


def inner_product(first, second):
    return jnp.sum(first.astype(jnp.float32) * second.astype(jnp.float32))


def axis_sum(value, axis):
    size = lax.axis_size(axis)
    if size & (size - 1):
        return lax.psum(value, axis)
    step = 1
    while step < size:
        pairs = [(i, i ^ step) for i in range(size)]
        value = value + lax.ppermute(value, axis, pairs)
        step *= 2
    return value


def global_sums(values):
    for axis in ("mode", "ty", "tx"):
        values = axis_sum(values, axis)
    return values


def folded(value, axis, dim, width):
    size, length = (lax.axis_size(axis), value.shape[dim])
    up = [(i, (i + 1) % size) for i in range(size)]
    down = [(j, i) for i, j in up]
    first = lax.slice_in_dim(value, 0, width, axis=dim)
    last = lax.slice_in_dim(value, length - width, length, axis=dim)
    from_before = lax.ppermute(last, axis, up)
    from_after = lax.ppermute(first, axis, down)
    inner = lax.slice_in_dim(value, width, length - width, axis=dim)
    edge = inner.shape[dim]
    head = lax.slice_in_dim(inner, 0, width, axis=dim) + from_before
    middle = lax.slice_in_dim(inner, width, edge - width, axis=dim)
    tail = lax.slice_in_dim(inner, edge - width, edge, axis=dim) + from_after
    return jnp.concatenate([head, middle, tail], axis=dim)


def direction_search(gradient, past_steps, past_changes, portion):
    memory = past_steps.shape[0]
    steps = portion(past_steps).astype(jnp.float32)
    changes = portion(past_changes).astype(jnp.float32)
    part = portion(gradient)
    cells = (1, 2, 3, 4)
    terms = []
    for index in range(memory):
        terms.append(jnp.sum(steps[index][None] * changes, axis=cells))
    for index in range(memory):
        terms.append(jnp.sum(changes[index][None] * changes, axis=cells))
    terms.append(jnp.sum(steps * part[None], axis=cells))
    terms.append(jnp.sum(changes * part[None], axis=cells))
    totals = global_sums(jnp.stack(terms))
    cross, square = (totals[:memory], totals[memory : 2 * memory])
    with_steps, with_changes = (totals[2 * memory], totals[2 * memory + 1])
    alphas = [None] * memory
    for i in reversed(range(memory)):
        value = with_steps[i]
        for j in reversed(range(i + 1, memory)):
            value = value - alphas[j] * cross[i, j]
        alphas[i] = value / cross[i, i]
    scaling = cross[memory - 1, memory - 1] / square[memory - 1, memory - 1]
    gammas = []
    for i in range(memory):
        value = with_changes[i]
        for j in reversed(range(memory)):
            value = value - alphas[j] * square[j, i]
        value = scaling * value
        for j in range(i):
            value = value + gammas[j] * cross[j, i]
        gammas.append(alphas[i] - value / cross[i, i])
    search = gradient
    for i in reversed(range(memory)):
        search = search - alphas[i] * past_changes[i].astype(jnp.float32)
    search = scaling * search
    for i in range(memory):
        search = search + gammas[i] * past_steps[i].astype(jnp.float32)
    return search


def per_device(object_field, probe, patterns, offsets, phase, past_steps, past_changes):
    slice_count = object_field.shape[0]
    tile_edge = object_field.shape[2]
    probe_edge = probe.shape[1]
    mode_index = lax.axis_index("mode")
    mode_count = lax.axis_size("mode")
    tables = dft_tables(probe_edge)
    kernel = jnp.concatenate([jnp.cos(phase), jnp.sin(phase)], -1)
    extended = extended_2(object_field, (("ty", 2), ("tx", 3)), HALO)
    pattern_index = 0
    starts = (0, 0, offsets[pattern_index, 0], offsets[pattern_index, 1])
    window = lax.dynamic_slice(extended, starts, (slice_count, 2, probe_edge, probe_edge))
    window_list = [jnp.concatenate([window[:, 0], window[:, 1]], -1)]
    windows = jnp.stack(window_list, 0)
    far_field, entering = forward_waves(windows, probe, kernel, tables)
    partial_intensity = jnp.sum(
        far_field[..., :probe_edge] ** 2 + far_field[..., probe_edge:] ** 2, axis=1
    )
    intensity = axis_sum(partial_intensity, "mode") / MODES
    residual = intensity - patterns
    pieces = window_gradients(far_field, entering, windows, residual, kernel, tables)
    extended_edge = tile_edge + 2 * HALO
    collected = jnp.zeros((slice_count, 2, extended_edge, extended_edge), jnp.float32)
    pattern_index = 0
    piece_now = pieces[pattern_index]
    unpacked = jnp.stack([piece_now[..., :probe_edge], piece_now[..., probe_edge:]], 1)
    starts = (0, 0, offsets[pattern_index, 0], offsets[pattern_index, 1])
    collected = lax.dynamic_update_slice(collected, unpacked, starts)
    tile_gradient = folded(folded(collected, "ty", 2, HALO), "tx", 3, HALO)
    share_rows = tile_edge // mode_count

    def own_rows(array):
        return lax.dynamic_slice_in_dim(array, mode_index * share_rows, share_rows, array.ndim - 2)

    gradient = tile_gradient + REG_WEIGHT * object_field
    search = direction_search(gradient, past_steps, past_changes, own_rows)
    return (object_field - search, gradient)


def solution(mesh):
    placed = (
        P(None, None, "ty", "tx"),
        P("mode", None, None),
        P(("ty", "tx"), None, None),
        P(("ty", "tx"), None),
        P(),
        P(None, None, None, "ty", "tx"),
        P(None, None, None, "ty", "tx"),
    )
    return jax.shard_map(
        per_device,
        mesh=mesh,
        in_specs=placed,
        out_specs=(P(None, None, "ty", "tx"), P(None, None, "ty", "tx")),
        check_vma=False,
    )
```
